512 devices in a mesh: tensor: 4 (over x), context: 8 (over y, core), dp: 16 (over z).
Axes of the slice: x: 4, y: 4, z: 16, core: 2. Of those that a mesh axis runs over, the one named last changes fastest.
Arguments:
- tokens: bfloat16 [32768, 3584], P(('tensor', 'context'), 'dp'), may hold values from -6 to 6
- route_ids: int32 [32768, 1], P(('tensor', 'context')), may hold values from 0 to 31; in each aligned block of 1024 rows (0 to 1023, 1024 to 2047, ...) at most 48 rows name the same one
- route_weights: float32 [32768, 1], P(('tensor', 'context')), may hold values from 0.2 to 1
- cotangent: bfloat16 [32768, 3584], P(('tensor', 'context'), 'dp'), may hold values from -6 to 6
- w_gate: bfloat16 [32, 2560, 3584], P(('tensor', 'context'), 'dp'), may hold values from -0.09375 to 0.09375
- w_up: bfloat16 [32, 2560, 3584], P(('tensor', 'context'), 'dp'), may hold values from -0.09375 to 0.09375
- w_down: bfloat16 [32, 3584, 2560], P(('tensor', 'context'), 'dp'), may hold values from -0.125 to 0.125
Outputs:
- mixed: bfloat16 [32768, 3584], P(('tensor', 'context'), 'dp')
- route_grad: float32 [32768, 1], P(('tensor', 'context'))
The draws below stay inside these ranges and needn't reach their ends.
Inputs may be any that keep to these rules, and one draw needn't show every extreme that they name: `route_ids`: each row names one expert. In each aligned block of 1024 rows (the rows of one index of tensor+context) no expert is named by more than 48 routes, and in every draw some expert is named by exactly 48 routes of some block.
All inputs are finite; a program needn't handle non-finite values.
Results may differ from the reference program's by a relative error of at most 0.0057.
Values may be sent and summed in bfloat16 or wider, within the bound.
A program may use at most 64 MiB of HBM per device.

```python
import math
import jax
import jax.numpy as jnp
import numpy as np
from jax import lax

D = 3584
HID = 2560
TOP = 1
TOK_DEV = 1024
EXPERTS = 32
TOKENS = 32768
CAP = 48


def level_of(rng, extent, cuts, smallest, high):
    loudness = 1.0
    for axis_at, parts in cuts:
        steps = jax.random.uniform(jax.random.fold_in(jax.random.fold_in(rng, 6), axis_at), (parts,), jnp.float32, smallest / len(cuts), high / len(cuts))
        loudness = loudness * jnp.repeat(jnp.exp(steps), extent[axis_at] // parts).reshape((-1,) + (1,) * (len(extent) - 1 - axis_at))
    return loudness


def assign_block(stream_key, own, number, rows, count, top, limit, slope):
    ranking = jax.random.permutation(stream_key, count)
    heavy_load, ordinary = portions_of(count, rows * top, limit, slope, True), portions_of(count, rows * top, limit, slope, False)
    places = jnp.arange(count)

    def named(tallies, turn):
        used = int((tallies > 0).sum())
        fixed = max(1, used // 4)
        passed = fixed + (places - fixed + turn * (used - fixed)) % max(1, count - fixed)
        return jnp.zeros((count,), jnp.int32).at[ranking[jnp.where(places < fixed, places, passed)]].set(jnp.asarray(tallies, jnp.int32))

    tallies = jnp.where(number % 4 == 0, named(heavy_load, number // 4), named(ordinary, number - number // 4 - 1))
    mixed = jax.random.permutation(jax.random.fold_in(own, 3), count)
    source_of, sink = mixed[0:count // 2 * 2:2], mixed[1:count // 2 * 2:2]
    room = jnp.minimum(tallies[source_of] - 1, limit - tallies[sink]) // 2
    room = jnp.where((source_of == ranking[0]) | (sink == ranking[0]) | (tallies[sink] == 0), 0, jnp.maximum(room, 0))
    passed = jax.random.randint(jax.random.fold_in(own, 4), (count // 2,), 0, 1 << 20) % (room + 1)
    tallies = tallies.at[source_of].add(-passed).at[sink].add(passed)
    items = jnp.searchsorted(jnp.cumsum(tallies), jnp.arange(rows * top), side="right").astype(jnp.int32)
    listing = items.reshape(top, rows).T
    listing = listing[jax.random.permutation(jax.random.fold_in(own, 1), rows)]
    turn = jax.random.randint(jax.random.fold_in(own, 2), (rows, 1), 0, top)
    return jnp.take_along_axis(listing, (jnp.arange(top)[None, :] + turn) % top, axis=1)


def portions_of(count, total, bound, lean, full):
    loads = [(1 << 20) // math.isqrt(grade ** lean) + 1 for grade in range(1, count + 1)]
    largest = bound if full else min(bound, max(-(-total // count), total * loads[0] // sum(loads)))
    least = 1 if total - largest >= count - 1 else 0
    holding, rest = [largest] + [least] * (count - 1), total - largest - least * (count - 1)
    while rest > 0:
        candidates = [i for i in range(1, count) if holding[i] < largest] or [i for i in range(1, count) if holding[i] < bound]
        whole, budget = sum([loads[i] for i in candidates]), rest
        for i in candidates:
            addition = min(bound - holding[i], max(1, budget * loads[i] // whole), rest)
            holding[i] = holding[i] + addition
            rest = rest - addition
    return np.array(holding)


def normal_values(stream_key, dims, scale, most, pieces=(), held_as=jnp.bfloat16):
    gain = level_of(stream_key, dims, pieces, -0.22, 0.18) if pieces else 1.0
    array = jax.random.normal(stream_key, dims, jnp.float32) * scale * gain
    return jnp.minimum(jnp.maximum(array, -most), most).astype(held_as)


def setup_inputs(seed: int = 0) -> dict:
    arg_keys = jax.random.split(jax.random.key(seed), 8)
    tokens = normal_values(arg_keys[0], (TOKENS, D), 1.0, 6.0, ((0, 32), (1, 16)))
    route_ids_keys = jax.random.split(jax.random.fold_in(arg_keys[1], 1), TOKENS // TOK_DEV)
    route_ids_turns = jax.random.permutation(jax.random.fold_in(arg_keys[1], 3), TOKENS // TOK_DEV)
    route_ids = jax.vmap(lambda own, number: assign_block(jax.random.fold_in(arg_keys[1], 2), own, number, TOK_DEV, EXPERTS, TOP, CAP, 2))(route_ids_keys, route_ids_turns).reshape((TOKENS, TOP))
    route_weights = jnp.clip(0.2 + 0.8 * jax.random.uniform(arg_keys[2], (TOKENS, TOP), jnp.float32) ** level_of(arg_keys[2], (TOKENS, TOP), ((0, 32),), -0.2, 0.2), 0.2, 1.0)
    cotangent = normal_values(arg_keys[3], (TOKENS, D), 1.0, 6.0, ((0, 32), (1, 16)))
    w_gate = normal_values(arg_keys[4], (EXPERTS, HID, D), D ** -0.5, 0.09375, ((0, 32), (1, 16)))
    w_up = normal_values(arg_keys[5], (EXPERTS, HID, D), D ** -0.5, 0.09375, ((0, 32), (1, 16)))
    w_down = normal_values(arg_keys[6], (EXPERTS, D, HID), HID ** -0.5, 0.125, ((0, 32), (1, 16)))
    return {"tokens": tokens, "route_ids": route_ids, "route_weights": route_weights, "cotangent": cotangent, "w_gate": w_gate, "w_up": w_up, "w_down": w_down}


def expert_pass(items):
    token_rows, gate_w, up_w, down_w = items
    contract = (((1,), (1,)), ((), ()))
    gate = lax.dot_general(token_rows, gate_w, contract, preferred_element_type=jnp.float32)
    up = lax.dot_general(token_rows, up_w, contract, preferred_element_type=jnp.float32)
    hidden = (gate * jax.nn.sigmoid(gate) * up).astype(jnp.bfloat16)
    return lax.dot_general(hidden, down_w, contract, preferred_element_type=jnp.float32).astype(jnp.bfloat16)


def reference(tokens, route_ids, route_weights, cotangent, w_gate, w_up, w_down):
    per_expert = EXPERTS * CAP
    pair_count = TOKENS * TOP
    blocks = route_ids.reshape(EXPERTS, TOK_DEV * TOP)
    onehot = (blocks[:, :, None] == jnp.arange(EXPERTS, dtype=jnp.int32)[None, None, :]).astype(jnp.int32)
    before = jnp.cumsum(onehot, axis=1) - onehot
    position = jnp.sum(onehot * before, axis=2)
    owner = jnp.arange(EXPERTS, dtype=jnp.int32)[:, None] * CAP
    slot = (blocks * per_expert + owner + position).reshape(pair_count).astype(jnp.int32)
    token_pairs = jnp.repeat(tokens, TOP, axis=0)
    cot_pairs = jnp.repeat(cotangent, TOP, axis=0).astype(jnp.float32)
    weight_flat = route_weights.reshape(pair_count, 1)
    token_slots = jnp.zeros((EXPERTS * per_expert, D), jnp.bfloat16).at[slot].set(token_pairs)
    expert_out = lax.map(expert_pass, (token_slots.reshape(EXPERTS, per_expert, D), w_gate, w_up, w_down))
    out_pairs = expert_out.reshape(EXPERTS * per_expert, D)[slot].astype(jnp.float32)
    mixed = jnp.sum((weight_flat * out_pairs).reshape(TOKENS, TOP, D), axis=1).astype(jnp.bfloat16)
    route_grad = (jnp.sum(out_pairs * cot_pairs, axis=1) * D ** -0.5).reshape(TOKENS, TOP)
    return mixed, route_grad
```

```python
import jax
import jax.numpy as jnp
from jax import lax
from jax.experimental import pallas as pl
from jax.experimental.pallas import tpu as pltpu
from jax.sharding import PartitionSpec as P

MESH = pl.DeviceIdType.MESH
F32, BF16 = jnp.float32, jnp.bfloat16
NX, NC, NZ = 4, 8, 16
ROWS, FEAT, HID, D = 1024, 224, 160, 3584
CAP = 48
XSLOTS = NC * CAP
GX = 2
GROUP = GX * XSLOTS
GROUPS = NX // GX
TILE = 128
NT = (((1,), (1,)), ((), ()))
TOK_PIECES = ((0, 64), (64, 48), (112, 64), (176, 48))
HID_PIECES = ((0, 48), (48, 32), (80, 48), (128, 32))
PIECES = len(TOK_PIECES)
UP_LAST = range(PIECES // 2)
DOWN_LAST = range(PIECES // 2, PIECES)


def kernel(
    ids_ref, wts_ref, tok_in, cot_ref, wg_hbm, wu_hbm, wd_hbm,
    mix_ref, route_ref,
    wg, wu, wd, place, xs, xr, tok, hid, outs, ret, pairs, parts,
    w_sem, x_send, x_recv, t_send, t_recv, h_send, h_recv, o_send, o_recv, p_send, p_recv,
):
    mx, mc, mz = lax.axis_index("tensor"), lax.axis_index("context"), lax.axis_index("dp")
    above, below = lax.rem(mz + 1, NZ), lax.rem(mz + NZ - 1, NZ)

    barrier = pltpu.get_barrier_semaphore()

    def greet(k, carry):
        p = lax.rem(mx * NC + mc + k, NX * NC)
        pl.semaphore_signal(barrier, inc=1, device_id=(p // NC, lax.rem(p, NC), mz), device_id_type=MESH)
        return carry

    def greet_z(k, carry):
        pl.semaphore_signal(barrier, inc=1, device_id=(mx, mc, lax.rem(mz + k, NZ)), device_id_type=MESH)
        return carry

    lax.fori_loop(1, NX * NC, greet, 0)
    lax.fori_loop(1, NZ, greet_z, 0)
    loads = [
        pltpu.make_async_copy(src, dst, w_sem.at[i])
        for i, (src, dst) in enumerate(((wg_hbm, wg), (wu_hbm, wu), (wd_hbm, wd)))
    ]
    for load in loads:
        load.start()

    ids = ids_ref[...]
    rel = lax.rem(mx + NX - ids // NC, NX) * NC + lax.rem(ids, NC)
    expert = lax.broadcasted_iota(jnp.int32, (NX * NC, TILE), 0)
    lower = (
        lax.broadcasted_iota(jnp.int32, (TILE, TILE), 0) < lax.broadcasted_iota(jnp.int32, (TILE, TILE), 1)
    ).astype(F32).astype(BF16)
    seen = jnp.zeros((NX * NC, 1), F32)
    slots = []
    for i in range(ROWS // TILE):
        r = rel[:, i * TILE : (i + 1) * TILE]
        onehot = (expert == r).astype(F32)
        before = jnp.dot(onehot.astype(BF16), lower, preferred_element_type=F32) + seen
        position = jnp.sum(onehot * before, axis=0, keepdims=True)
        slots.append(r * CAP + position.astype(jnp.int32))
        seen = seen + jnp.sum(onehot, axis=1, keepdims=True)
    slot = jnp.concatenate(slots, axis=1)

    def place_rows(j):
        at = lax.broadcasted_iota(jnp.int32, (XSLOTS, ROWS), 0) + j * XSLOTS
        rows = pl.ds(j * XSLOTS, XSLOTS)
        place[rows, :] = (at == slot).astype(F32).astype(BF16)
        xs[rows, :] = lax.dot_general(place[rows, :], tok_in[...], NT, preferred_element_type=F32).astype(BF16)

    def piece_at(j, c):
        return pl.ds(pl.multiple_of((j * NC + c) * CAP, 16), CAP)

    def scatter(src, dst, send, recv, j, toward):
        tx = lax.rem(mx + NX + toward * j, NX)

        def one(k, carry):
            c = lax.rem(mc + k, NC)
            pltpu.make_async_remote_copy(
                src_ref=src.at[piece_at(j, c), :],
                dst_ref=dst.at[piece_at(j, mc), :],
                send_sem=send,
                recv_sem=recv.at[j // GX],
                device_id=(tx, c, mz),
                device_id_type=MESH,
            ).start()
            return carry

        if j == 0:
            pltpu.make_async_copy(src.at[piece_at(0, mc), :], dst.at[piece_at(0, mc), :], recv.at[0]).start()
        lax.fori_loop(1 if j == 0 else 0, NC, one, 0)

    def scattered(dst, recv, g):
        part = dst.at[pl.ds(g * GROUP, GROUP), :]
        pltpu.make_async_copy(part, part, recv.at[g]).wait()

    def all_sent(buf, send):
        part = buf.at[pl.ds(CAP, (NX * NC - 1) * CAP), :]
        pltpu.make_async_copy(part, part, send).wait()

    def ring(buf, send, recv, pieces, g, way, s, p):
        origin = lax.rem(mz + NZ - s, NZ) if way == 0 else lax.rem(mz + s, NZ)
        start, size = pieces[p]
        part = buf.at[g, origin, pl.ds(start, size), :]
        return pltpu.make_async_remote_copy(
            src_ref=part,
            dst_ref=part,
            send_sem=send.at[g],
            recv_sem=recv.at[g, way, s, p],
            device_id=(mx, mc, above if way == 0 else below),
            device_id_type=MESH,
        )

    def arrived(buf, send, recv, pieces, g, way, s, p):
        origin = lax.rem(mz + NZ - s, NZ) if way == 0 else lax.rem(mz + s, NZ)
        start, size = pieces[p]
        part = buf.at[g, origin, pl.ds(start, size), :]
        pltpu.make_async_copy(part, part, recv.at[g, way, s - 1, p]).wait()

    def begin(phase):
        for p in range(PIECES):
            for way in range(2):
                ring(*phase, way, 0, p).start()

    def run(phase, work, after):
        def step(s, carry):
            for p in range(PIECES):
                for way in range(2):
                    arrived(*phase, way, s, p)
                    ring(*phase, way, s, p).start()
            work(s - 1)
            return carry

        lax.fori_loop(1, NZ // 2 - 1, step, 0)
        s = NZ // 2 - 1
        for p in range(PIECES):
            for way in range(2):
                arrived(*phase, way, s, p)
                if p in (UP_LAST if way == 0 else DOWN_LAST):
                    ring(*phase, way, s, p).start()
        after()
        for p in range(PIECES // 2):
            arrived(*phase, 0, NZ // 2, UP_LAST[p])
            arrived(*phase, 1, NZ // 2, DOWN_LAST[p])

    def ring_sent(phase):
        buf, send, _, _, g = phase
        part = buf.at[g, pl.ds(0, NZ - 1)]
        pltpu.make_async_copy(part, part, send.at[g]).wait()

    tok_phase = [(tok, t_send, t_recv, TOK_PIECES, g) for g in range(GROUPS)]
    hid_phase = [(hid, h_send, h_recv, HID_PIECES, g) for g in range(GROUPS)]

    def turn_in(g):
        tok[g, mz] = xr[pl.ds(g * GROUP, GROUP), :].astype(F32).T.astype(BF16)

    def expert_in(g, i):
        cols = pl.ds(pl.multiple_of(i * TILE, TILE), TILE)
        x = tok[g, :, :, cols].reshape(NZ * FEAT, TILE)
        gate = jnp.dot(wg[...], x, preferred_element_type=F32)
        up = jnp.dot(wu[...], x, preferred_element_type=F32)
        hid[g, mz, :, cols] = (gate * jax.nn.sigmoid(gate) * up).astype(BF16)

    def expert_out(g, i):
        cols = pl.ds(pl.multiple_of(i * TILE, TILE), TILE)
        h = hid[g, :, :, cols].reshape(NZ * HID, TILE)
        out = jnp.dot(wd[...], h, preferred_element_type=F32).astype(BF16).astype(F32)
        outs[pl.ds(pl.multiple_of(g * GROUP + i * TILE, TILE), TILE), :] = out.T.astype(BF16)

    def unplace(g):
        rows = pl.ds(g * GROUP, GROUP)
        got = ret[rows, :].astype(F32).T.astype(BF16)
        return jnp.dot(got, place[rows, :], preferred_element_type=F32)

    pl.semaphore_wait(barrier, NX * NC - 1 + NZ - 1)
    for j in range(NX):
        place_rows(j)
        scatter(xs, xr, x_send, x_recv, j, -1)
    scattered(xr, x_recv, 0)
    turn_in(0)
    begin(tok_phase[0])
    scattered(xr, x_recv, 1)
    turn_in(1)
    for load in loads:
        load.wait()

    run(tok_phase[0], lambda i: None, lambda: begin(tok_phase[1]))
    run(tok_phase[1], lambda i: expert_in(0, i), lambda: begin(hid_phase[0]))
    run(hid_phase[0], lambda i: expert_in(1, i), lambda: begin(hid_phase[1]))

    def send_back(g):
        for j in range(g * GX, (g + 1) * GX):
            scatter(outs, ret, o_send, o_recv, j, 1)

    run(hid_phase[1], lambda i: expert_out(0, i), lambda: send_back(0))

    def tail(i, carry):
        expert_out(1, i)
        return carry

    lax.fori_loop(0, GROUP // TILE, tail, 0)
    send_back(1)
    scattered(ret, o_recv, 0)
    pairs[...] = unplace(0)
    scattered(ret, o_recv, 1)
    pairs[...] += unplace(1)
    for i in range(ROWS // TILE):
        cols = pl.ds(i * TILE, TILE)
        parts[mz, pl.ds(i, 1), :] = jnp.sum(pairs[:, cols] * cot_ref[:, cols].astype(F32), axis=0, keepdims=True)

    def share(k, carry):
        pltpu.make_async_remote_copy(
            src_ref=parts.at[mz],
            dst_ref=parts.at[mz],
            send_sem=p_send,
            recv_sem=p_recv,
            device_id=(mx, mc, lax.rem(mz + k, NZ)),
            device_id_type=MESH,
        ).start()
        return carry

    lax.fori_loop(1, NZ, share, 0)
    mix_ref[...] = (pairs[...] * wts_ref[...]).astype(BF16)
    all_sent(xs, x_send)
    all_sent(outs, o_send)
    for phase in tok_phase + hid_phase:
        ring_sent(phase)
    others = parts.at[pl.ds(0, NZ - 1)]
    pltpu.make_async_copy(others, others, p_recv).wait()
    pltpu.make_async_copy(others, others, p_send).wait()
    route_ref[...] = jnp.sum(parts[...], axis=0) * D ** (-0.5)


def per_device(tokens, route_ids, route_weights, cotangent, w_gate, w_up, w_down):
    vmem, hbm = pl.BlockSpec(memory_space=pltpu.VMEM), pl.BlockSpec(memory_space=pl.ANY)
    dma, slots = pltpu.SemaphoreType.DMA, NX * NC * CAP
    mixed, route = pl.pallas_call(
        kernel,
        out_shape=(jax.ShapeDtypeStruct((FEAT, ROWS), BF16), jax.ShapeDtypeStruct((8, TILE), F32)),
        in_specs=[vmem] * 4 + [hbm] * 3,
        out_specs=(vmem, vmem),
        scratch_shapes=[
            pltpu.VMEM((HID, D), BF16),
            pltpu.VMEM((HID, D), BF16),
            pltpu.VMEM((FEAT, NZ * HID), BF16),
            pltpu.VMEM((slots, ROWS), BF16),
            pltpu.VMEM((slots, FEAT), BF16),
            pltpu.VMEM((slots, FEAT), BF16),
            pltpu.VMEM((GROUPS, NZ, FEAT, GROUP), BF16),
            pltpu.VMEM((GROUPS, NZ, HID, GROUP), BF16),
            pltpu.VMEM((slots, FEAT), BF16),
            pltpu.VMEM((slots, FEAT), BF16),
            pltpu.VMEM((FEAT, ROWS), F32),
            pltpu.VMEM((NZ, 8, TILE), F32),
            dma((3,)),
            dma,
            dma((GROUPS,)),
            dma((GROUPS,)),
            dma((GROUPS, 2, NZ // 2, PIECES)),
            dma((GROUPS,)),
            dma((GROUPS, 2, NZ // 2, PIECES)),
            dma,
            dma((GROUPS,)),
            dma,
            dma,
        ],
        compiler_params=pltpu.CompilerParams(
            collective_id=0, has_side_effects=True, vmem_limit_bytes=52 * 2**20
        ),
    )(
        route_ids.reshape(1, ROWS),
        route_weights.reshape(1, ROWS),
        tokens.T,
        cotangent.T,
        w_gate[0],
        w_up[0],
        w_down[0],
    )
    return mixed.T, route.reshape(ROWS, 1)


def solution(mesh):
    in_specs = (
        P(("tensor", "context"), "dp"),
        P(("tensor", "context"), None),
        P(("tensor", "context"), None),
        P(("tensor", "context"), "dp"),
        P(("tensor", "context"), "dp", None),
        P(("tensor", "context"), "dp", None),
        P(("tensor", "context"), "dp", None),
    )
    out_specs = (P(("tensor", "context"), "dp"), P(("tensor", "context"), None))
    return jax.shard_map(
        per_device, mesh=mesh, in_specs=in_specs, out_specs=out_specs, check_vma=False
    )
```

```python
import jax
import jax.numpy as jnp
from jax import lax
from jax.experimental import pallas as pl
from jax.experimental.pallas import tpu as pltpu
from jax.sharding import PartitionSpec as P

MESH = pl.DeviceIdType.MESH
F32, BF16 = jnp.float32, jnp.bfloat16
NX, NC, NZ = 4, 8, 16
ROWS, FEAT, HID, D = 1024, 224, 160, 3584
CAP = 48
XSLOTS = NC * CAP
GX = 2
GROUP = GX * XSLOTS
GROUPS = NX // GX
SLOTS = NX * XSLOTS
TILE = 128
NT = (((1,), (1,)), ((), ()))
PLAIN = 128
SLOTTED = FEAT - PLAIN
PAIR = 2 * PLAIN
STEPS = NZ // 2
FAR = (STEPS - 1) * PAIR
PLAIN_PIECES = tuple((32 * p, 32, 0, ROWS) for p in range(4))
SLOTTED_PIECES = tuple((48 * (p % 2), 48, GROUP * (p // 2), GROUP) for p in range(4))
HID_PIECES = tuple((80 * (p % 2), 80, XSLOTS * (p // 2), XSLOTS) for p in range(4))
PIECES = 4


def kernel(
    ids_ref, wts_ref, tok_in, cot_ref, wg_hbm, wu_hbm, wd_hbm,
    mix_ref, route_ref,
    wg, wu, wd, w_placed, w_slot, place, xs, xr, ps, pr, plain, slotted, acc, hid, outs, ret, pairs, parts,
    w_sem, x_send, x_recv, ps_send, ps_recv, a_send, a_recv, b_send, b_recv, h_send, h_recv,
    o_send, o_recv, p_send, p_recv,
):
    mx, mc, mz = lax.axis_index("tensor"), lax.axis_index("context"), lax.axis_index("dp")
    above, below = lax.rem(mz + 1, NZ), lax.rem(mz + NZ - 1, NZ)

    barrier = pltpu.get_barrier_semaphore()

    def greet(k, carry):
        p = lax.rem(mx * NC + mc + k, NX * NC)
        pl.semaphore_signal(barrier, inc=1, device_id=(p // NC, lax.rem(p, NC), mz), device_id_type=MESH)
        return carry

    def greet_z(k, carry):
        pl.semaphore_signal(barrier, inc=1, device_id=(mx, mc, lax.rem(mz + k, NZ)), device_id_type=MESH)
        return carry

    lax.fori_loop(1, NZ, greet_z, 0)
    lax.fori_loop(1, NX * NC, greet, 0)
    loads = [
        pltpu.make_async_copy(src, dst, w_sem.at[i])
        for i, (src, dst) in enumerate(((wg_hbm, wg), (wu_hbm, wu), (wd_hbm, wd)))
    ]
    for load in loads:
        load.start()

    ids = ids_ref[...]
    rel = lax.rem(mx + NX - ids // NC, NX) * NC + lax.rem(ids, NC)
    expert = lax.broadcasted_iota(jnp.int32, (NX * NC, TILE), 0)
    lower = (
        lax.broadcasted_iota(jnp.int32, (TILE, TILE), 0) < lax.broadcasted_iota(jnp.int32, (TILE, TILE), 1)
    ).astype(F32).astype(BF16)
    seen = jnp.zeros((NX * NC, 1), F32)
    slots = []
    for i in range(ROWS // TILE):
        r = rel[:, i * TILE : (i + 1) * TILE]
        onehot = (expert == r).astype(F32)
        before = jnp.dot(onehot.astype(BF16), lower, preferred_element_type=F32) + seen
        position = jnp.sum(onehot * before, axis=0, keepdims=True)
        slots.append(r * CAP + position.astype(jnp.int32))
        seen = seen + jnp.sum(onehot, axis=1, keepdims=True)
    slot = jnp.concatenate(slots, axis=1)

    def piece_at(j, c):
        return pl.ds(pl.multiple_of((j * NC + c) * CAP, 16), CAP)

    def scatter(src, dst, send, recv, j, toward, lanes):
        tx = lax.rem(mx + NX + toward * j, NX)

        def one(k, carry):
            c = lax.rem(mc + k, NC)
            pltpu.make_async_remote_copy(
                src_ref=src.at[piece_at(j, c), lanes],
                dst_ref=dst.at[piece_at(j, mc), lanes],
                send_sem=send,
                recv_sem=recv,
                device_id=(tx, c, mz),
                device_id_type=MESH,
            ).start()
            return carry

        if j == 0:
            pltpu.make_async_copy(src.at[piece_at(0, mc), lanes], dst.at[piece_at(0, mc), lanes], recv).start()
        lax.fori_loop(1 if j == 0 else 0, NC, one, 0)

    def wait_for(part, sem):
        pltpu.make_async_copy(part, part, sem).wait()

    def offset_rows(j):
        return pl.ds(j * XSLOTS, XSLOTS)

    def group_rows(g):
        return pl.ds(g * GROUP, GROUP)

    def part_of(ring, way, s, p):
        origin = lax.rem(mz + NZ - s, NZ) if way == 0 else lax.rem(mz + s, NZ)
        r, rows, c, cols = ring["pieces"][p]
        return ring["buf"].at[(*ring["at"], origin, pl.ds(r, rows), pl.ds(c, cols))]

    def forward(ring, way, s, p):
        part = part_of(ring, way, s, p)
        src = part
        if isinstance(s, int) and s == 0 and "own" in ring:
            r, rows, c, cols = ring["pieces"][p]
            src = ring["own"].at[pl.ds(r, rows), pl.ds(c, cols)]
        pltpu.make_async_remote_copy(
            src_ref=src,
            dst_ref=part,
            send_sem=ring["send"],
            recv_sem=ring["recv"].at[(*ring["at"], way, s, p)],
            device_id=(mx, mc, above if way == 0 else below),
            device_id_type=MESH,
        ).start()

    def arrived(ring, way, s, p):
        wait_for(part_of(ring, way, s, p), ring["recv"].at[(*ring["at"], way, s - 1, p)])

    def begin(ring):
        for p in range(PIECES):
            for way in range(2):
                forward(ring, way, 0, p)

    def run(ring, work, after):
        def step(s, carry):
            for p in range(PIECES):
                for way in range(2):
                    arrived(ring, way, s, p)
                    forward(ring, way, s, p)
            work(s)
            return carry

        lax.fori_loop(1, STEPS - 1, step, 0)
        for p in range(PIECES):
            for way in range(2):
                arrived(ring, way, STEPS - 1, p)
                if p % 2 == way:
                    forward(ring, way, STEPS - 1, p)
        after()

    def last(ring, p):
        arrived(ring, p % 2, STEPS, p)

    def ring_sent(ring):
        wait_for(ring["buf"].at[(*ring["at"], pl.ds(0, NZ - 1))], ring["send"])

    plain_ring = dict(buf=plain, at=(), send=a_send, recv=a_recv, pieces=PLAIN_PIECES, own=tok_in)
    slotted_ring = dict(buf=slotted, at=(), send=b_send, recv=b_recv, pieces=SLOTTED_PIECES)
    hid_rings = [
        dict(buf=hid, at=(g,), send=h_send.at[g], recv=h_recv, pieces=HID_PIECES) for g in range(GROUPS)
    ]

    def put_own(j):
        rows = offset_rows(j)
        at = lax.broadcasted_iota(jnp.int32, (XSLOTS, ROWS), 0) + j * XSLOTS
        place[rows, :] = (at == slot).astype(F32).astype(BF16)
        xs[rows, :] = lax.dot_general(place[rows, :], tok_in[...], NT, preferred_element_type=F32).astype(BF16)
        scatter(xs, xr, x_send, x_recv.at[j // GX], j, -1, pl.ds(0, FEAT))

    def put_pair(j, s):
        lanes = pl.ds(pl.multiple_of((s - 1) * PAIR, PAIR), PAIR)
        rows = offset_rows(j)
        pair = jnp.concatenate([plain[lax.rem(mz + NZ - s, NZ)], plain[lax.rem(mz + s, NZ)]], axis=0)
        ps[rows, lanes] = lax.dot_general(place[rows, :], pair, NT, preferred_element_type=F32).astype(BF16)
        scatter(ps, pr, ps_send, ps_recv.at[j // GX], j, -1, lanes)

    def put_far(j):
        lanes = pl.ds(FAR, PLAIN)
        rows = offset_rows(j)
        far = plain[lax.rem(mz + STEPS, NZ)]
        ps[rows, lanes] = lax.dot_general(place[rows, :], far, NT, preferred_element_type=F32).astype(BF16)
        scatter(ps, pr, ps_send, ps_recv.at[j // GX], j, -1, lanes)

    def sort_weights(planes):
        for o in planes:
            away = lax.rem(o + NZ - mz, NZ)
            half = away // STEPS
            lane = lax.rem((1 - half) * (PAIR * away - PLAIN) + half * PAIR * (NZ - 1 - away) + NZ * PLAIN, NZ * PLAIN)
            at = pl.ds(pl.multiple_of(lane, TILE), PLAIN)
            for rows, w in ((pl.ds(0, HID), wg), (pl.ds(HID, HID), wu)):
                w_placed[rows, at] = w[:, o * FEAT : o * FEAT + PLAIN]
                w_slot[rows, o * SLOTTED : (o + 1) * SLOTTED] = w[:, o * FEAT + PLAIN : (o + 1) * FEAT]

    def turn_in(g):
        slotted[mz, :, g * GROUP : (g + 1) * GROUP] = xr[group_rows(g), pl.ds(PLAIN, SLOTTED)].astype(F32).T.astype(BF16)

    def placed_in(g, i):
        start = pl.multiple_of(g * GROUP + i * TILE, TILE)
        rows, cols = pl.ds(start, TILE), pl.ds(start, TILE)
        acc[:, cols] = lax.dot_general(
            w_placed[:, pl.ds(0, FAR + PLAIN)], pr[rows, :], NT, preferred_element_type=F32
        ) + lax.dot_general(
            w_placed[:, pl.ds(FAR + PLAIN, PLAIN)], xr[rows, pl.ds(0, PLAIN)], NT, preferred_element_type=F32
        )

    def slotted_in(g, i):
        start = pl.multiple_of(g * GROUP + i * TILE, TILE)
        cols = pl.ds(start, TILE)
        x = slotted[:, :, cols].reshape(NZ * SLOTTED, TILE)
        both = acc[:, cols] + jnp.dot(w_slot[...], x, preferred_element_type=F32)
        gate, up = both[:HID], both[HID:]
        hid[g, mz, :, pl.ds(pl.multiple_of(i * TILE, TILE), TILE)] = (gate * jax.nn.sigmoid(gate) * up).astype(BF16)

    def expert_out(g, i):
        cols = pl.ds(pl.multiple_of(i * TILE, TILE), TILE)
        h = hid[g, :, :, cols].reshape(NZ * HID, TILE)
        out = jnp.dot(wd[...], h, preferred_element_type=F32).astype(BF16).astype(F32)
        outs[pl.ds(pl.multiple_of(g * GROUP + i * TILE, TILE), TILE), :] = out.T.astype(BF16)

    def send_back(j):
        scatter(outs, ret, o_send, o_recv.at[j], j, 1, pl.ds(0, FEAT))

    def unplace(j):
        rows = offset_rows(j)
        wait_for(ret.at[rows, :], o_recv.at[j])
        got = ret[rows, :].astype(F32).T.astype(BF16)
        return jnp.dot(got, place[rows, :], preferred_element_type=F32)

    def each(n, f):
        def one(i, carry):
            f(i)
            return carry

        lax.fori_loop(0, n, one, 0)

    tiles = GROUP // TILE
    pl.semaphore_wait(barrier, NX * NC - 1 + NZ - 1)

    begin(plain_ring)
    for j in range(NX):
        put_own(j)

    def plain_work(s):
        for j in range(GX):
            put_pair(j, s)

        @pl.when(s == 1)
        def _():
            for load in loads:
                load.wait()

        for k in range(STEPS - 2):
            @pl.when(s == k + 1)
            def _():
                sort_weights(range(NZ * k // (STEPS - 2), NZ * (k + 1) // (STEPS - 2)))

        @pl.when(s == 4)
        def _():
            for g in range(GROUPS):
                wait_for(xr.at[group_rows(g), :], x_recv.at[g])
                turn_in(g)

    run(plain_ring, plain_work, lambda: begin(slotted_ring))
    for j in range(GX):
        put_pair(j, STEPS - 1)
    for p in range(PIECES):
        last(plain_ring, p)
    for j in range(NX):
        put_far(j)

    def slotted_work(s):
        for j in range(GX, NX):
            put_pair(j, s)

        @pl.when(s == 4)
        def _():
            wait_for(pr.at[group_rows(0), :], ps_recv.at[0])

        @pl.when(s >= 4)
        def _():
            placed_in(0, 2 * (s - 4))
            placed_in(0, 2 * (s - 4) + 1)

    run(slotted_ring, slotted_work, lambda: None)
    for p in range(2):
        last(slotted_ring, p)
    each(tiles, lambda i: slotted_in(0, i))
    begin(hid_rings[0])
    for j in range(GX, NX):
        put_pair(j, STEPS - 1)
    for p in range(2, PIECES):
        last(slotted_ring, p)

    def hid_work_0(s):
        @pl.when(s == 3)
        def _():
            wait_for(pr.at[group_rows(1), :], ps_recv.at[1])

        @pl.when(s >= 3)
        def _():
            i = s - 3
            placed_in(1, i)
            slotted_in(1, i)

    def hid_after_0():
        for i in range(STEPS - 4, tiles):
            placed_in(1, i)
            slotted_in(1, i)
        begin(hid_rings[1])

    run(hid_rings[0], hid_work_0, hid_after_0)
    for p in range(PIECES):
        last(hid_rings[0], p)

    def hid_work_1(s):
        @pl.when(s <= 3)
        def _():
            expert_out(0, 2 * s - 2)
            expert_out(0, 2 * s - 1)

        @pl.when(s == 4)
        def _():
            for j in range(GX):
                send_back(j)

        @pl.when(s == 6)
        def _():
            pairs[...] = unplace(0) + unplace(1)

    run(hid_rings[1], hid_work_1, lambda: None)
    for j in range(GX):
        for p in range(2 * j, 2 * j + 2):
            last(hid_rings[1], p)
        each(tiles // GX, lambda i: expert_out(1, j * (tiles // GX) + i))
        send_back(GX + j)
    pairs[...] += unplace(2)
    pairs[...] += unplace(3)
    for i in range(ROWS // TILE):
        cols = pl.ds(i * TILE, TILE)
        parts[mz, pl.ds(i, 1), :] = jnp.sum(pairs[:, cols] * cot_ref[:, cols].astype(F32), axis=0, keepdims=True)

    def share(k, carry):
        pltpu.make_async_remote_copy(
            src_ref=parts.at[mz],
            dst_ref=parts.at[mz],
            send_sem=p_send,
            recv_sem=p_recv,
            device_id=(mx, mc, lax.rem(mz + k, NZ)),
            device_id_type=MESH,
        ).start()
        return carry

    lax.fori_loop(1, NZ, share, 0)
    mix_ref[...] = (pairs[...] * wts_ref[...]).astype(BF16)
    own = pl.ds(CAP, SLOTS - CAP)
    wait_for(xs.at[own, :], x_send)
    wait_for(ps.at[own, :], ps_send)
    wait_for(outs.at[own, :], o_send)
    for ring in [plain_ring, slotted_ring] + hid_rings:
        ring_sent(ring)
    others = parts.at[pl.ds(0, NZ - 1)]
    wait_for(others, p_recv)
    wait_for(others, p_send)
    route_ref[...] = jnp.sum(parts[...], axis=0) * D ** (-0.5)


def per_device(tokens, route_ids, route_weights, cotangent, w_gate, w_up, w_down):
    vmem, hbm = pl.BlockSpec(memory_space=pltpu.VMEM), pl.BlockSpec(memory_space=pl.ANY)
    dma = pltpu.SemaphoreType.DMA
    ring_sems = (2, STEPS, PIECES)
    mixed, route = pl.pallas_call(
        kernel,
        out_shape=(jax.ShapeDtypeStruct((FEAT, ROWS), BF16), jax.ShapeDtypeStruct((8, TILE), F32)),
        in_specs=[vmem] * 4 + [hbm] * 3,
        out_specs=(vmem, vmem),
        scratch_shapes=[
            pltpu.VMEM((HID, D), BF16),
            pltpu.VMEM((HID, D), BF16),
            pltpu.VMEM((FEAT, NZ * HID), BF16),
            pltpu.VMEM((2 * HID, NZ * PLAIN), BF16),
            pltpu.VMEM((2 * HID, NZ * SLOTTED), BF16),
            pltpu.VMEM((SLOTS, ROWS), BF16),
            pltpu.VMEM((SLOTS, FEAT), BF16),
            pltpu.VMEM((SLOTS, FEAT), BF16),
            pltpu.VMEM((SLOTS, FAR + PLAIN), BF16),
            pltpu.VMEM((SLOTS, FAR + PLAIN), BF16),
            pltpu.VMEM((NZ, PLAIN, ROWS), BF16),
            pltpu.VMEM((NZ, SLOTTED, SLOTS), BF16),
            pltpu.VMEM((2 * HID, SLOTS), F32),
            pltpu.VMEM((GROUPS, NZ, HID, GROUP), BF16),
            pltpu.VMEM((SLOTS, FEAT), BF16),
            pltpu.VMEM((SLOTS, FEAT), BF16),
            pltpu.VMEM((FEAT, ROWS), F32),
            pltpu.VMEM((NZ, 8, TILE), F32),
            dma((3,)),
            dma,
            dma((GROUPS,)),
            dma,
            dma((GROUPS,)),
            dma,
            dma(ring_sems),
            dma,
            dma(ring_sems),
            dma((GROUPS,)),
            dma((GROUPS, *ring_sems)),
            dma,
            dma((NX,)),
            dma,
            dma,
        ],
        compiler_params=pltpu.CompilerParams(
            collective_id=0, has_side_effects=True, vmem_limit_bytes=60 * 2**20
        ),
    )(
        route_ids.reshape(1, ROWS),
        route_weights.reshape(1, ROWS),
        tokens.T,
        cotangent.T,
        w_gate[0],
        w_up[0],
        w_down[0],
    )
    return mixed.T, route.reshape(ROWS, 1)


def solution(mesh):
    in_specs = (
        P(("tensor", "context"), "dp"),
        P(("tensor", "context"), None),
        P(("tensor", "context"), None),
        P(("tensor", "context"), "dp"),
        P(("tensor", "context"), "dp", None),
        P(("tensor", "context"), "dp", None),
        P(("tensor", "context"), "dp", None),
    )
    out_specs = (P(("tensor", "context"), "dp"), P(("tensor", "context"), None))
    return jax.shard_map(
        per_device, mesh=mesh, in_specs=in_specs, out_specs=out_specs, check_vma=False
    )
```

```python
import jax
import jax.numpy as jnp
from jax import lax
from jax.experimental import pallas as pl
from jax.experimental.pallas import tpu as pltpu
from jax.sharding import PartitionSpec as P

MESH = pl.DeviceIdType.MESH
F32, BF16 = jnp.float32, jnp.bfloat16
NX, NC, NZ = 4, 8, 16
OFFSETS = (0, 2, 1, 3)
ROWS, FEAT, HID, D = 1024, 224, 160, 3584
CAP = 48
XSLOTS = NC * CAP
GX = 2
GROUP = GX * XSLOTS
GROUPS = NX // GX
SLOTS = NX * XSLOTS
TILE = 128
NT = (((1,), (1,)), ((), ()))
PLAIN = 128
SLOTTED = FEAT - PLAIN
PAIR = 2 * PLAIN
STEPS = NZ // 2
FAR = (STEPS - 1) * PAIR
PLAIN_PIECES = tuple((32 * p, 32, 0, ROWS) for p in range(4))
SLOTTED_PIECES = tuple((48 * (p % 2), 48, GROUP * (p // 2), GROUP) for p in range(4))
HID_PIECES = tuple((80 * (p % 2), 80, XSLOTS * (p // 2), XSLOTS) for p in range(4))
PIECES = 4


def kernel(
    ids_ref, wts_ref, tok_in, cot_ref, wg_hbm, wu_hbm, wd_hbm,
    mix_ref, route_ref,
    wg, wu, wd, w_placed, w_slot, place, xs, xr, ps, pr, plain, slotted, acc, hid, outs, ret, pairs, parts,
    w_sem, x_send, x_recv, ps_send, ps_recv, a_send, a_recv, b_send, b_recv, h_send, h_recv,
    o_send, o_recv, p_send, p_recv,
):
    mx, mc, mz = lax.axis_index("tensor"), lax.axis_index("context"), lax.axis_index("dp")
    above, below = lax.rem(mz + 1, NZ), lax.rem(mz + NZ - 1, NZ)

    barrier = pltpu.get_barrier_semaphore()

    def greet(k, carry):
        p = lax.rem(mx * NC + mc + k, NX * NC)
        pl.semaphore_signal(barrier, inc=1, device_id=(p // NC, lax.rem(p, NC), mz), device_id_type=MESH)
        return carry

    for plane in (above, below):
        pl.semaphore_signal(barrier, inc=1, device_id=(mx, mc, plane), device_id_type=MESH)
    lax.fori_loop(1, NX * NC, greet, 0)
    loads = [
        pltpu.make_async_copy(src, dst, w_sem.at[i])
        for i, (src, dst) in enumerate(((wg_hbm, wg), (wu_hbm, wu), (wd_hbm, wd)))
    ]
    for load in loads:
        load.start()

    def piece_at(j, c):
        return pl.ds(pl.multiple_of((j * NC + c) * CAP, 16), CAP)

    def scatter(src, dst, send, recv, j, toward, lanes):
        tx = lax.rem(mx + NX + toward * OFFSETS[j], NX)

        def one(k, carry):
            c = lax.rem(mc + k, NC)
            pltpu.make_async_remote_copy(
                src_ref=src.at[piece_at(j, c), lanes],
                dst_ref=dst.at[piece_at(j, mc), lanes],
                send_sem=send,
                recv_sem=recv,
                device_id=(tx, c, mz),
                device_id_type=MESH,
            ).start()
            return carry

        if j == 0:
            pltpu.make_async_copy(src.at[piece_at(0, mc), lanes], dst.at[piece_at(0, mc), lanes], recv).start()
        lax.fori_loop(1 if j == 0 else 0, NC, one, 0)

    def wait_for(part, sem):
        pltpu.make_async_copy(part, part, sem).wait()

    def offset_rows(j):
        return pl.ds(j * XSLOTS, XSLOTS)

    def group_rows(g):
        return pl.ds(g * GROUP, GROUP)

    def part_of(ring, way, s, p):
        origin = lax.rem(mz + NZ - s, NZ) if way == 0 else lax.rem(mz + s, NZ)
        r, rows, c, cols = ring["pieces"][p]
        return ring["buf"].at[(*ring["at"], origin, pl.ds(r, rows), pl.ds(c, cols))]

    def forward(ring, way, s, p):
        part = part_of(ring, way, s, p)
        src = part
        if isinstance(s, int) and s == 0 and "own" in ring:
            r, rows, c, cols = ring["pieces"][p]
            src = ring["own"].at[pl.ds(r, rows), pl.ds(c, cols)]
        pltpu.make_async_remote_copy(
            src_ref=src,
            dst_ref=part,
            send_sem=ring["send"],
            recv_sem=ring["recv"].at[(*ring["at"], way, s, p)],
            device_id=(mx, mc, above if way == 0 else below),
            device_id_type=MESH,
        ).start()

    def arrived(ring, way, s, p):
        wait_for(part_of(ring, way, s, p), ring["recv"].at[(*ring["at"], way, s - 1, p)])

    def begin(ring):
        for p in range(PIECES):
            for way in range(2):
                forward(ring, way, 0, p)

    def run(ring, work, after):
        def step(s, carry):
            for p in range(PIECES):
                for way in range(2):
                    arrived(ring, way, s, p)
                    forward(ring, way, s, p)
            work(s)
            return carry

        lax.fori_loop(1, STEPS - 1, step, 0)
        for p in range(PIECES):
            for way in range(2):
                arrived(ring, way, STEPS - 1, p)
                if p % 2 == way:
                    forward(ring, way, STEPS - 1, p)
        after()

    def last(ring, p):
        arrived(ring, p % 2, STEPS, p)

    def ring_sent(ring):
        wait_for(ring["buf"].at[(*ring["at"], pl.ds(0, NZ - 1))], ring["send"])

    plain_ring = dict(buf=plain, at=(), send=a_send, recv=a_recv, pieces=PLAIN_PIECES, own=tok_in)
    slotted_ring = dict(buf=slotted, at=(), send=b_send, recv=b_recv, pieces=SLOTTED_PIECES)
    hid_rings = [
        dict(buf=hid, at=(g,), send=h_send.at[g], recv=h_recv, pieces=HID_PIECES) for g in range(GROUPS)
    ]

    def put_own(j):
        rows = offset_rows(j)
        at = lax.broadcasted_iota(jnp.int32, (XSLOTS, ROWS), 0) + j * XSLOTS
        place[rows, :] = (at == slot).astype(F32).astype(BF16)
        xs[rows, :] = lax.dot_general(place[rows, :], tok_in[...], NT, preferred_element_type=F32).astype(BF16)
        scatter(xs, xr, x_send, x_recv.at[j // GX], j, -1, pl.ds(0, FEAT))

    def put_pair(j, s):
        lanes = pl.ds(pl.multiple_of((s - 1) * PAIR, PAIR), PAIR)
        rows = offset_rows(j)
        pair = jnp.concatenate([plain[lax.rem(mz + NZ - s, NZ)], plain[lax.rem(mz + s, NZ)]], axis=0)
        ps[rows, lanes] = lax.dot_general(place[rows, :], pair, NT, preferred_element_type=F32).astype(BF16)
        scatter(ps, pr, ps_send, ps_recv.at[j // GX], j, -1, lanes)

    def put_far(j):
        lanes = pl.ds(FAR, PLAIN)
        rows = offset_rows(j)
        far = plain[lax.rem(mz + STEPS, NZ)]
        ps[rows, lanes] = lax.dot_general(place[rows, :], far, NT, preferred_element_type=F32).astype(BF16)
        scatter(ps, pr, ps_send, ps_recv.at[j // GX], j, -1, lanes)

    def sort_weights(planes):
        for o in planes:
            away = lax.rem(o + NZ - mz, NZ)
            half = away // STEPS
            lane = lax.rem((1 - half) * (PAIR * away - PLAIN) + half * PAIR * (NZ - 1 - away) + NZ * PLAIN, NZ * PLAIN)
            at = pl.ds(pl.multiple_of(lane, TILE), PLAIN)
            for rows, w in ((pl.ds(0, HID), wg), (pl.ds(HID, HID), wu)):
                w_placed[rows, at] = w[:, o * FEAT : o * FEAT + PLAIN]
                w_slot[rows, o * SLOTTED : (o + 1) * SLOTTED] = w[:, o * FEAT + PLAIN : (o + 1) * FEAT]

    def turn_in(g):
        slotted[mz, :, g * GROUP : (g + 1) * GROUP] = xr[group_rows(g), pl.ds(PLAIN, SLOTTED)].astype(F32).T.astype(BF16)

    def placed_in(g, i):
        start = pl.multiple_of(g * GROUP + i * TILE, TILE)
        rows, cols = pl.ds(start, TILE), pl.ds(start, TILE)
        acc[:, cols] = lax.dot_general(
            w_placed[:, pl.ds(0, FAR + PLAIN)], pr[rows, :], NT, preferred_element_type=F32
        ) + lax.dot_general(
            w_placed[:, pl.ds(FAR + PLAIN, PLAIN)], xr[rows, pl.ds(0, PLAIN)], NT, preferred_element_type=F32
        )

    def slotted_in(g, i, width=TILE):
        start = pl.multiple_of(g * GROUP + i * width, TILE)
        cols = pl.ds(start, width)
        x = slotted[:, :, cols].reshape(NZ * SLOTTED, width)
        both = acc[:, cols] + jnp.dot(w_slot[...], x, preferred_element_type=F32)
        gate, up = both[:HID], both[HID:]
        hid[g, mz, :, pl.ds(pl.multiple_of(i * width, TILE), width)] = (gate * jax.nn.sigmoid(gate) * up).astype(BF16)

    def expert_out(g, i, width=TILE):
        cols = pl.ds(pl.multiple_of(i * width, TILE), width)
        h = hid[g, :, :, cols].reshape(NZ * HID, width)
        out = jnp.dot(wd[...], h, preferred_element_type=F32).astype(BF16).astype(F32)
        outs[pl.ds(pl.multiple_of(g * GROUP + i * width, TILE), width), :] = out.T.astype(BF16)

    def send_back(j):
        scatter(outs, ret, o_send, o_recv.at[j], j, 1, pl.ds(0, FEAT))

    def unplace(j):
        rows = offset_rows(j)
        wait_for(ret.at[rows, :], o_recv.at[j])
        got = ret[rows, :].astype(F32).T.astype(BF16)
        return jnp.dot(got, place[rows, :], preferred_element_type=F32)

    tiles = GROUP // TILE
    pl.semaphore_wait(barrier, NX * NC - 1 + 2)

    begin(plain_ring)
    ids = ids_ref[...]
    offset = lax.rem(mx + NX - ids // NC, NX)
    rel = (lax.rem(offset, 2) * 2 + offset // 2) * NC + lax.rem(ids, NC)
    expert = lax.broadcasted_iota(jnp.int32, (NX * NC, TILE), 0)
    lower = (
        lax.broadcasted_iota(jnp.int32, (TILE, TILE), 0) < lax.broadcasted_iota(jnp.int32, (TILE, TILE), 1)
    ).astype(F32).astype(BF16)
    seen = jnp.zeros((NX * NC, 1), F32)
    slots = []
    for i in range(ROWS // TILE):
        r = rel[:, i * TILE : (i + 1) * TILE]
        onehot = (expert == r).astype(F32)
        before = jnp.dot(onehot.astype(BF16), lower, preferred_element_type=F32) + seen
        position = jnp.sum(onehot * before, axis=0, keepdims=True)
        slots.append(r * CAP + position.astype(jnp.int32))
        seen = seen + jnp.sum(onehot, axis=1, keepdims=True)
    slot = jnp.concatenate(slots, axis=1)
    for j in range(NX):
        put_own(j)

    def plain_work(s):
        for j in range(GX):
            put_pair(j, s)

        @pl.when(s == 1)
        def _():
            for load in loads:
                load.wait()

        for k in range(STEPS - 2):
            @pl.when(s == k + 1)
            def _():
                sort_weights(range(NZ * k // (STEPS - 2), NZ * (k + 1) // (STEPS - 2)))

        @pl.when(s == 4)
        def _():
            for g in range(GROUPS):
                wait_for(xr.at[group_rows(g), :], x_recv.at[g])
                turn_in(g)

    run(plain_ring, plain_work, lambda: begin(slotted_ring))
    for j in range(GX):
        put_pair(j, STEPS - 1)
    for p in range(PIECES):
        last(plain_ring, p)
    for j in range(NX):
        put_far(j)

    def slotted_work(s):
        for j in range(GX, NX):
            put_pair(j, s)

        @pl.when(s == 4)
        def _():
            wait_for(pr.at[group_rows(0), :], ps_recv.at[0])

        @pl.when(s >= 4)
        def _():
            placed_in(0, 2 * (s - 4))
            placed_in(0, 2 * (s - 4) + 1)

    run(slotted_ring, slotted_work, lambda: None)
    for p in range(2):
        last(slotted_ring, p)
    for half in range(GX):
        slotted_in(0, half, XSLOTS)
        for p in range(2 * half, 2 * half + 2):
            for way in range(2):
                forward(hid_rings[0], way, 0, p)
    for j in range(GX, NX):
        put_pair(j, STEPS - 1)
    for p in range(2, PIECES):
        last(slotted_ring, p)

    def hid_work_0(s):
        @pl.when(s == 3)
        def _():
            wait_for(pr.at[group_rows(1), :], ps_recv.at[1])

        @pl.when(s >= 3)
        def _():
            i = s - 3
            placed_in(1, i)
            slotted_in(1, i)

    def hid_after_0():
        for i in range(STEPS - 4, tiles):
            placed_in(1, i)
            slotted_in(1, i)
        begin(hid_rings[1])

    run(hid_rings[0], hid_work_0, hid_after_0)
    for p in range(PIECES):
        last(hid_rings[0], p)

    def hid_work_1(s):
        @pl.when(s <= 3)
        def _():
            expert_out(0, 2 * s - 2)
            expert_out(0, 2 * s - 1)

        @pl.when(s == 4)
        def _():
            for j in range(GX):
                send_back(j)

        @pl.when(s == 6)
        def _():
            pairs[...] = unplace(0) + unplace(1)

    run(hid_rings[1], hid_work_1, lambda: None)
    for j in range(GX):
        for p in range(2 * j, 2 * j + 2):
            last(hid_rings[1], p)
        expert_out(1, j, XSLOTS)
        send_back(GX + j)
    pairs[...] += unplace(2)
    pairs[...] += unplace(3)
    for i in range(ROWS // TILE):
        cols = pl.ds(i * TILE, TILE)
        parts[mz, pl.ds(i, 1), :] = jnp.sum(pairs[:, cols] * cot_ref[:, cols].astype(F32), axis=0, keepdims=True)

    def share(k, carry):
        pltpu.make_async_remote_copy(
            src_ref=parts.at[mz],
            dst_ref=parts.at[mz],
            send_sem=p_send,
            recv_sem=p_recv,
            device_id=(mx, mc, lax.rem(mz + k, NZ)),
            device_id_type=MESH,
        ).start()
        return carry

    lax.fori_loop(1, NZ, share, 0)
    mix_ref[...] = (pairs[...] * wts_ref[...]).astype(BF16)
    own = pl.ds(CAP, SLOTS - CAP)
    wait_for(xs.at[own, :], x_send)
    wait_for(ps.at[own, :], ps_send)
    wait_for(outs.at[own, :], o_send)
    for ring in [plain_ring, slotted_ring] + hid_rings:
        ring_sent(ring)
    others = parts.at[pl.ds(0, NZ - 1)]
    wait_for(others, p_recv)
    wait_for(others, p_send)
    route_ref[...] = jnp.sum(parts[...], axis=0) * D ** (-0.5)


def hand_over(mix_in, route_in, mix_out, route_out):
    mix_out[...] = mix_in[...]
    route_out[...] = route_in[...]


def per_device(tokens, route_ids, route_weights, cotangent, w_gate, w_up, w_down):
    vmem, hbm = pl.BlockSpec(memory_space=pltpu.VMEM), pl.BlockSpec(memory_space=pl.ANY)
    dma = pltpu.SemaphoreType.DMA
    ring_sems = (2, STEPS, PIECES)
    out_shape = (jax.ShapeDtypeStruct((FEAT, ROWS), BF16), jax.ShapeDtypeStruct((8, TILE), F32))
    results = pl.pallas_call(
        kernel,
        out_shape=out_shape,
        in_specs=[vmem] * 4 + [hbm] * 3,
        out_specs=(vmem, vmem),
        scratch_shapes=[
            pltpu.VMEM((HID, D), BF16),
            pltpu.VMEM((HID, D), BF16),
            pltpu.VMEM((FEAT, NZ * HID), BF16),
            pltpu.VMEM((2 * HID, NZ * PLAIN), BF16),
            pltpu.VMEM((2 * HID, NZ * SLOTTED), BF16),
            pltpu.VMEM((SLOTS, ROWS), BF16),
            pltpu.VMEM((SLOTS, FEAT), BF16),
            pltpu.VMEM((SLOTS, FEAT), BF16),
            pltpu.VMEM((SLOTS, FAR + PLAIN), BF16),
            pltpu.VMEM((SLOTS, FAR + PLAIN), BF16),
            pltpu.VMEM((NZ, PLAIN, ROWS), BF16),
            pltpu.VMEM((NZ, SLOTTED, SLOTS), BF16),
            pltpu.VMEM((2 * HID, SLOTS), F32),
            pltpu.VMEM((GROUPS, NZ, HID, GROUP), BF16),
            pltpu.VMEM((SLOTS, FEAT), BF16),
            pltpu.VMEM((SLOTS, FEAT), BF16),
            pltpu.VMEM((FEAT, ROWS), F32),
            pltpu.VMEM((NZ, 8, TILE), F32),
            dma((3,)),
            dma,
            dma((GROUPS,)),
            dma,
            dma((GROUPS,)),
            dma,
            dma(ring_sems),
            dma,
            dma(ring_sems),
            dma((GROUPS,)),
            dma((GROUPS, *ring_sems)),
            dma,
            dma((NX,)),
            dma,
            dma,
        ],
        compiler_params=pltpu.CompilerParams(
            collective_id=0, has_side_effects=True, vmem_limit_bytes=60 * 2**20
        ),
    )(
        route_ids.reshape(1, ROWS),
        route_weights.reshape(1, ROWS),
        tokens.T,
        cotangent.T,
        w_gate[0],
        w_up[0],
        w_down[0],
    )
    mixed, route = pl.pallas_call(
        hand_over,
        out_shape=out_shape,
        in_specs=[vmem] * 2,
        out_specs=(vmem, vmem),
    )(*results)
    return mixed.T, route.reshape(ROWS, 1)


def solution(mesh):
    in_specs = (
        P(("tensor", "context"), "dp"),
        P(("tensor", "context"), None),
        P(("tensor", "context"), None),
        P(("tensor", "context"), "dp"),
        P(("tensor", "context"), "dp", None),
        P(("tensor", "context"), "dp", None),
        P(("tensor", "context"), "dp", None),
    )
    out_specs = (P(("tensor", "context"), "dp"), P(("tensor", "context"), None))
    return jax.shard_map(
        per_device, mesh=mesh, in_specs=in_specs, out_specs=out_specs, check_vma=False
    )
```

```python
import jax
import jax.numpy as jnp
from jax import lax
from jax.experimental import pallas as pl
from jax.experimental.pallas import tpu as pltpu
from jax.sharding import PartitionSpec as P

MESH = pl.DeviceIdType.MESH
F32, BF16 = jnp.float32, jnp.bfloat16
NX, NC, NZ = 4, 8, 16
OFFSETS = (1, 3, 2, 0)
ROWS, FEAT, HID, D = 1024, 224, 160, 3584
CAP = 48
XSLOTS = NC * CAP
GX = 2
GROUP = GX * XSLOTS
GROUPS = NX // GX
SLOTS = NX * XSLOTS
TILE = 128
NT = (((1,), (1,)), ((), ()))
PLAIN = 128
SLOTTED = FEAT - PLAIN
PAIR = 2 * PLAIN
STEPS = NZ // 2
FAR = (STEPS - 1) * PAIR
PLAIN_PIECES = tuple((32 * p, 32, 0, ROWS) for p in range(4))
SLOTTED_PIECES = tuple((48 * (p % 2), 48, GROUP * (p // 2), GROUP) for p in range(4))
HID_PIECES = tuple((80 * (p % 2), 80, XSLOTS * (p // 2), XSLOTS) for p in range(4))
PIECES = 4


def kernel(
    ids_ref, wts_ref, tok_hbm, cot_hbm, wg_hbm, wu_hbm, wd_hbm,
    mix_ref, route_ref,
    tok_in, cot_ref, wg, wu, wd, w_placed, w_slot, place, xs, xr, ps, pr, plain, slotted, acc, hid, outs, ret, pairs, parts,
    w_sem, x_send, x_recv, ps_send, ps_recv, a_send, a_recv, b_send, b_recv, h_send, h_recv,
    o_send, o_recv, p_send, p_recv,
):
    mx, mc, mz = lax.axis_index("tensor"), lax.axis_index("context"), lax.axis_index("dp")
    above, below = lax.rem(mz + 1, NZ), lax.rem(mz + NZ - 1, NZ)

    barrier = pltpu.get_barrier_semaphore()

    def greet(k, carry):
        p = lax.rem(mx * NC + mc + k, NX * NC)
        pl.semaphore_signal(barrier, inc=1, device_id=(p // NC, lax.rem(p, NC), mz), device_id_type=MESH)
        return carry

    for plane in (above, below):
        pl.semaphore_signal(barrier, inc=1, device_id=(mx, mc, plane), device_id_type=MESH)
    lax.fori_loop(1, NX * NC, greet, 0)
    loads = [
        pltpu.make_async_copy(src, dst, w_sem.at[i])
        for i, (src, dst) in enumerate(((tok_hbm, tok_in), (wg_hbm, wg), (wu_hbm, wu), (wd_hbm, wd), (cot_hbm, cot_ref)))
    ]
    for load in loads:
        load.start()

    def piece_at(j, c):
        return pl.ds(pl.multiple_of((j * NC + c) * CAP, 16), CAP)

    def scatter(src, dst, send, recv, j, toward, lanes):
        tx = lax.rem(mx + NX + toward * OFFSETS[j], NX)

        def one(k, carry):
            c = lax.rem(mc + k, NC)
            pltpu.make_async_remote_copy(
                src_ref=src.at[piece_at(j, c), lanes],
                dst_ref=dst.at[piece_at(j, mc), lanes],
                send_sem=send,
                recv_sem=recv,
                device_id=(tx, c, mz),
                device_id_type=MESH,
            ).start()
            return carry

        here = OFFSETS[j] == 0
        if here:
            pltpu.make_async_copy(src.at[piece_at(j, mc), lanes], dst.at[piece_at(j, mc), lanes], recv).start()
        lax.fori_loop(int(here), NC, one, 0)

    def wait_for(part, sem):
        pltpu.make_async_copy(part, part, sem).wait()

    def offset_rows(j):
        return pl.ds(j * XSLOTS, XSLOTS)

    def group_rows(g):
        return pl.ds(g * GROUP, GROUP)

    def part_of(ring, way, s, p):
        origin = lax.rem(mz + NZ - s, NZ) if way == 0 else lax.rem(mz + s, NZ)
        r, rows, c, cols = ring["pieces"][p]
        return ring["buf"].at[(*ring["at"], origin, pl.ds(r, rows), pl.ds(c, cols))]

    def forward(ring, way, s, p):
        part = part_of(ring, way, s, p)
        src = part
        if isinstance(s, int) and s == 0 and "own" in ring:
            r, rows, c, cols = ring["pieces"][p]
            src = ring["own"].at[pl.ds(r, rows), pl.ds(c, cols)]
        pltpu.make_async_remote_copy(
            src_ref=src,
            dst_ref=part,
            send_sem=ring["send"],
            recv_sem=ring["recv"].at[(*ring["at"], way, s, p)],
            device_id=(mx, mc, above if way == 0 else below),
            device_id_type=MESH,
        ).start()

    def arrived(ring, way, s, p):
        wait_for(part_of(ring, way, s, p), ring["recv"].at[(*ring["at"], way, s - 1, p)])

    def begin(ring):
        for p in range(PIECES):
            for way in range(2):
                forward(ring, way, 0, p)

    def run(ring, work, after):
        def step(s, carry):
            for p in range(PIECES):
                for way in range(2):
                    arrived(ring, way, s, p)
                    forward(ring, way, s, p)
            work(s)
            return carry

        lax.fori_loop(1, STEPS - 1, step, 0)
        for p in range(PIECES):
            for way in range(2):
                arrived(ring, way, STEPS - 1, p)
                if p % 2 == way:
                    forward(ring, way, STEPS - 1, p)
        after()

    def last(ring, p):
        arrived(ring, p % 2, STEPS, p)

    def ring_sent(ring):
        wait_for(ring["buf"].at[(*ring["at"], pl.ds(0, NZ - 1))], ring["send"])

    plain_ring = dict(buf=plain, at=(), send=a_send, recv=a_recv, pieces=PLAIN_PIECES, own=tok_in)
    slotted_ring = dict(buf=slotted, at=(), send=b_send, recv=b_recv, pieces=SLOTTED_PIECES)
    hid_rings = [
        dict(buf=hid, at=(g,), send=h_send.at[g], recv=h_recv, pieces=HID_PIECES) for g in range(GROUPS)
    ]

    def put_own(j):
        rows = offset_rows(j)
        at = lax.broadcasted_iota(jnp.int32, (XSLOTS, ROWS), 0) + j * XSLOTS
        place[rows, :] = (at == slot).astype(F32).astype(BF16)
        xs[rows, :] = lax.dot_general(place[rows, :], tok_in[...], NT, preferred_element_type=F32).astype(BF16)
        scatter(xs, xr, x_send, x_recv.at[j // GX], j, -1, pl.ds(0, FEAT))

    def put_pair(j, s):
        lanes = pl.ds(pl.multiple_of((s - 1) * PAIR, PAIR), PAIR)
        rows = offset_rows(j)
        pair = jnp.concatenate([plain[lax.rem(mz + NZ - s, NZ)], plain[lax.rem(mz + s, NZ)]], axis=0)
        ps[rows, lanes] = lax.dot_general(place[rows, :], pair, NT, preferred_element_type=F32).astype(BF16)
        scatter(ps, pr, ps_send, ps_recv.at[j // GX], j, -1, lanes)

    def put_far(j):
        lanes = pl.ds(FAR, PLAIN)
        rows = offset_rows(j)
        far = plain[lax.rem(mz + STEPS, NZ)]
        ps[rows, lanes] = lax.dot_general(place[rows, :], far, NT, preferred_element_type=F32).astype(BF16)
        scatter(ps, pr, ps_send, ps_recv.at[j // GX], j, -1, lanes)

    def sort_weights(planes):
        for o in planes:
            away = lax.rem(o + NZ - mz, NZ)
            half = away // STEPS
            lane = lax.rem((1 - half) * (PAIR * away - PLAIN) + half * PAIR * (NZ - 1 - away) + NZ * PLAIN, NZ * PLAIN)
            at = pl.ds(pl.multiple_of(lane, TILE), PLAIN)
            for rows, w in ((pl.ds(0, HID), wg), (pl.ds(HID, HID), wu)):
                w_placed[rows, at] = w[:, o * FEAT : o * FEAT + PLAIN]
                w_slot[rows, o * SLOTTED : (o + 1) * SLOTTED] = w[:, o * FEAT + PLAIN : (o + 1) * FEAT]

    def turn_in(g):
        slotted[mz, :, g * GROUP : (g + 1) * GROUP] = xr[group_rows(g), pl.ds(PLAIN, SLOTTED)].astype(F32).T.astype(BF16)

    def placed_in(g, i):
        start = pl.multiple_of(g * GROUP + i * TILE, TILE)
        rows, cols = pl.ds(start, TILE), pl.ds(start, TILE)
        acc[:, cols] = lax.dot_general(
            w_placed[:, pl.ds(0, FAR + PLAIN)], pr[rows, :], NT, preferred_element_type=F32
        ) + lax.dot_general(
            w_placed[:, pl.ds(FAR + PLAIN, PLAIN)], xr[rows, pl.ds(0, PLAIN)], NT, preferred_element_type=F32
        )

    def slotted_in(g, i, width=TILE):
        start = pl.multiple_of(g * GROUP + i * width, TILE)
        cols = pl.ds(start, width)
        x = slotted[:, :, cols].reshape(NZ * SLOTTED, width)
        both = acc[:, cols] + jnp.dot(w_slot[...], x, preferred_element_type=F32)
        gate, up = both[:HID], both[HID:]
        hid[g, mz, :, pl.ds(pl.multiple_of(i * width, TILE), width)] = (gate * jax.nn.sigmoid(gate) * up).astype(BF16)

    def expert_out(g, i, width=TILE):
        cols = pl.ds(pl.multiple_of(i * width, TILE), width)
        h = hid[g, :, :, cols].reshape(NZ * HID, width)
        out = jnp.dot(wd[...], h, preferred_element_type=F32).astype(BF16).astype(F32)
        outs[pl.ds(pl.multiple_of(g * GROUP + i * width, TILE), width), :] = out.T.astype(BF16)

    def send_back(j):
        scatter(outs, ret, o_send, o_recv.at[j], j, 1, pl.ds(0, FEAT))

    def unplace(j):
        rows = offset_rows(j)
        wait_for(ret.at[rows, :], o_recv.at[j])
        got = ret[rows, :].astype(F32).T.astype(BF16)
        return jnp.dot(got, place[rows, :], preferred_element_type=F32)

    tiles = GROUP // TILE
    pl.semaphore_wait(barrier, NX * NC - 1 + 2)

    loads[0].wait()
    begin(plain_ring)
    ids = ids_ref[...]
    offset = lax.rem(mx + NX - ids // NC, NX)
    odd = lax.rem(offset, 2)
    rel = (odd * (offset // 2) + (1 - odd) * (NX - 1 - offset // 2)) * NC + lax.rem(ids, NC)
    expert = lax.broadcasted_iota(jnp.int32, (NX * NC, TILE), 0)
    lower = (
        lax.broadcasted_iota(jnp.int32, (TILE, TILE), 0) < lax.broadcasted_iota(jnp.int32, (TILE, TILE), 1)
    ).astype(F32).astype(BF16)
    seen = jnp.zeros((NX * NC, 1), F32)
    slots = []
    for i in range(ROWS // TILE):
        r = rel[:, i * TILE : (i + 1) * TILE]
        onehot = (expert == r).astype(F32)
        before = jnp.dot(onehot.astype(BF16), lower, preferred_element_type=F32) + seen
        position = jnp.sum(onehot * before, axis=0, keepdims=True)
        slots.append(r * CAP + position.astype(jnp.int32))
        seen = seen + jnp.sum(onehot, axis=1, keepdims=True)
    slot = jnp.concatenate(slots, axis=1)
    for j in range(GX):
        put_own(j)

    def plain_work(s):
        for j in range(GX):
            put_pair(j, s)
        for j in range(GX, NX):
            @pl.when(s == j - 1)
            def _():
                put_own(j)

        @pl.when(s == 1)
        def _():
            for load in loads[1:]:
                load.wait()

        for k in range(STEPS - 2):
            @pl.when(s == k + 1)
            def _():
                sort_weights(range(NZ * k // (STEPS - 2), NZ * (k + 1) // (STEPS - 2)))

        @pl.when(s == 6)
        def _():
            for g in range(GROUPS):
                wait_for(xr.at[group_rows(g), :], x_recv.at[g])
                turn_in(g)

    run(plain_ring, plain_work, lambda: begin(slotted_ring))
    for j in range(GX):
        put_pair(j, STEPS - 1)
    for p in range(PIECES):
        last(plain_ring, p)
    for j in range(NX):
        put_far(j)

    def slotted_work(s):
        for j in range(GX, NX):
            put_pair(j, s)

        @pl.when(s == 4)
        def _():
            wait_for(pr.at[group_rows(0), :], ps_recv.at[0])

        @pl.when(s >= 4)
        def _():
            placed_in(0, 2 * (s - 4))
            placed_in(0, 2 * (s - 4) + 1)

    run(slotted_ring, slotted_work, lambda: None)
    for p in range(2):
        last(slotted_ring, p)
    for half in range(GX):
        slotted_in(0, half, XSLOTS)
        for p in range(2 * half, 2 * half + 2):
            for way in range(2):
                forward(hid_rings[0], way, 0, p)
    for j in range(GX, NX):
        put_pair(j, STEPS - 1)
    for p in range(2, PIECES):
        last(slotted_ring, p)

    def hid_work_0(s):
        @pl.when(s == 3)
        def _():
            wait_for(pr.at[group_rows(1), :], ps_recv.at[1])

        @pl.when(s >= 3)
        def _():
            i = s - 3
            placed_in(1, i)
            slotted_in(1, i)

    def hid_after_0():
        for i in range(STEPS - 4, tiles):
            placed_in(1, i)
            slotted_in(1, i)
        begin(hid_rings[1])

    run(hid_rings[0], hid_work_0, hid_after_0)
    for p in range(PIECES):
        last(hid_rings[0], p)

    def hid_work_1(s):
        @pl.when(s <= 3)
        def _():
            expert_out(0, 2 * s - 2)
            expert_out(0, 2 * s - 1)

        @pl.when(s == 4)
        def _():
            for j in range(GX):
                send_back(j)

        @pl.when(s == 6)
        def _():
            pairs[...] = unplace(0) + unplace(1)

    run(hid_rings[1], hid_work_1, lambda: None)
    for j in range(GX):
        for p in range(2 * j, 2 * j + 2):
            last(hid_rings[1], p)
        expert_out(1, j, XSLOTS)
        send_back(GX + j)
    pairs[...] += unplace(2)
    pairs[...] += unplace(3)
    for i in range(ROWS // TILE):
        cols = pl.ds(i * TILE, TILE)
        parts[mz, pl.ds(i, 1), :] = jnp.sum(pairs[:, cols] * cot_ref[:, cols].astype(F32), axis=0, keepdims=True)

    def share(k, carry):
        pltpu.make_async_remote_copy(
            src_ref=parts.at[mz],
            dst_ref=parts.at[mz],
            send_sem=p_send,
            recv_sem=p_recv,
            device_id=(mx, mc, lax.rem(mz + k, NZ)),
            device_id_type=MESH,
        ).start()
        return carry

    lax.fori_loop(1, NZ, share, 0)
    mix_ref[...] = (pairs[...] * wts_ref[...]).astype(BF16)
    own = pl.ds(CAP, SLOTS - CAP)
    wait_for(xs.at[own, :], x_send)
    wait_for(ps.at[own, :], ps_send)
    wait_for(outs.at[own, :], o_send)
    for ring in [plain_ring, slotted_ring] + hid_rings:
        ring_sent(ring)
    others = parts.at[pl.ds(0, NZ - 1)]
    wait_for(others, p_recv)
    wait_for(others, p_send)
    route_ref[...] = jnp.sum(parts[...], axis=0) * D ** (-0.5)


def hand_over(mix_in, route_in, mix_out, route_out):
    mix_out[...] = mix_in[...]
    route_out[...] = route_in[...]


def per_device(tokens, route_ids, route_weights, cotangent, w_gate, w_up, w_down):
    vmem, hbm = pl.BlockSpec(memory_space=pltpu.VMEM), pl.BlockSpec(memory_space=pl.ANY)
    dma = pltpu.SemaphoreType.DMA
    ring_sems = (2, STEPS, PIECES)
    out_shape = (jax.ShapeDtypeStruct((FEAT, ROWS), BF16), jax.ShapeDtypeStruct((8, TILE), F32))
    results = pl.pallas_call(
        kernel,
        out_shape=out_shape,
        in_specs=[vmem] * 2 + [hbm] * 5,
        out_specs=(vmem, vmem),
        scratch_shapes=[
            pltpu.VMEM((FEAT, ROWS), BF16),
            pltpu.VMEM((FEAT, ROWS), BF16),
            pltpu.VMEM((HID, D), BF16),
            pltpu.VMEM((HID, D), BF16),
            pltpu.VMEM((FEAT, NZ * HID), BF16),
            pltpu.VMEM((2 * HID, NZ * PLAIN), BF16),
            pltpu.VMEM((2 * HID, NZ * SLOTTED), BF16),
            pltpu.VMEM((SLOTS, ROWS), BF16),
            pltpu.VMEM((SLOTS, FEAT), BF16),
            pltpu.VMEM((SLOTS, FEAT), BF16),
            pltpu.VMEM((SLOTS, FAR + PLAIN), BF16),
            pltpu.VMEM((SLOTS, FAR + PLAIN), BF16),
            pltpu.VMEM((NZ, PLAIN, ROWS), BF16),
            pltpu.VMEM((NZ, SLOTTED, SLOTS), BF16),
            pltpu.VMEM((2 * HID, SLOTS), F32),
            pltpu.VMEM((GROUPS, NZ, HID, GROUP), BF16),
            pltpu.VMEM((SLOTS, FEAT), BF16),
            pltpu.VMEM((SLOTS, FEAT), BF16),
            pltpu.VMEM((FEAT, ROWS), F32),
            pltpu.VMEM((NZ, 8, TILE), F32),
            dma((5,)),
            dma,
            dma((GROUPS,)),
            dma,
            dma((GROUPS,)),
            dma,
            dma(ring_sems),
            dma,
            dma(ring_sems),
            dma((GROUPS,)),
            dma((GROUPS, *ring_sems)),
            dma,
            dma((NX,)),
            dma,
            dma,
        ],
        compiler_params=pltpu.CompilerParams(
            collective_id=0, has_side_effects=True, vmem_limit_bytes=60 * 2**20
        ),
    )(
        route_ids.reshape(1, ROWS),
        route_weights.reshape(1, ROWS),
        tokens.T,
        cotangent.T,
        w_gate[0],
        w_up[0],
        w_down[0],
    )
    mixed, route = pl.pallas_call(
        hand_over,
        out_shape=out_shape,
        in_specs=[vmem] * 2,
        out_specs=(vmem, vmem),
    )(*results)
    return mixed.T, route.reshape(ROWS, 1)


def solution(mesh):
    in_specs = (
        P(("tensor", "context"), "dp"),
        P(("tensor", "context"), None),
        P(("tensor", "context"), None),
        P(("tensor", "context"), "dp"),
        P(("tensor", "context"), "dp", None),
        P(("tensor", "context"), "dp", None),
        P(("tensor", "context"), "dp", None),
    )
    out_specs = (P(("tensor", "context"), "dp"), P(("tensor", "context"), None))
    return jax.shard_map(
        per_device, mesh=mesh, in_specs=in_specs, out_specs=out_specs, check_vma=False
    )
```
